128 devices in a mesh: island: 4 (over x_lo, core), fsdp: 16 (over y, z), tp: 2 (over x_hi).
Axes of the slice: x: 4 (x_hi: 2, x_lo: 2; x = x_hi * 2 + x_lo), y: 4, z: 4, core: 2. Of those that a mesh axis runs over, the one named last changes fastest.
Arguments:
- local_weights: bfloat16 [4, 4, 1024, 12288], P('island', None, 'fsdp', 'tp'), may hold values from -6 to 6
- outer_base: bfloat16 [3, 1024, 12288], P(None, 'fsdp', 'tp'), may hold values from -6 to 6
- momentum: float32 [3, 1024, 12288], P(None, 'fsdp', 'tp'), may hold values from -6 to 6
- layer_order: int32 [4], replicated, may hold values from 0 to 3, each once
- features: bfloat16 [4, 8192, 12288], P('island', 'fsdp', 'tp'), may hold values from -6 to 6
- targets: bfloat16 [4, 8192, 1024], P('island', 'fsdp'), may hold values from -6 to 6
Outputs:
- new_base: bfloat16 [3, 1024, 12288], P(None, 'fsdp', 'tp')
- new_momentum: float32 [3, 1024, 12288], P(None, 'fsdp', 'tp')
- inner_grad: float32 [4, 1024, 12288], P('island', 'fsdp', 'tp')
The draws below stay inside these ranges and needn't reach their ends.
Inputs may be any that keep to these rules, and one draw needn't show every extreme that they name: `layer_order`: a permutation of the window's layers.
All inputs are finite; a program needn't handle non-finite values. Where the reference program divides by a largest or mean magnitude, that divisor is 1e-20 or more.
Results may differ from the reference program's by a relative error of at most 0.024.
Values may be sent and summed in bfloat16 or wider, within the bound.
A program may use at most 128 MiB of HBM per device.

```python
import jax
import jax.numpy as jnp
from jax import lax

D = 12288
KW = 1024
LAYERS = 4
FRAG = 3
QB = 32
TOK_DEV = 512
TOKENS = 8192
ISLANDS = 4
N_FSDP = 16


def level_of(key, extent, shards, low, largest):
    gain, own = 1.0, jax.random.fold_in(key, 6)
    for position, parts in shards:
        steps = jnp.exp(jax.random.uniform(jax.random.fold_in(own, position), (parts,), jnp.float32, low / len(shards), largest / len(shards)))
        gain = gain * jnp.repeat(steps, extent[position] // parts).reshape([-1 if axis == position else 1 for axis in range(len(extent))])
    return gain


def normal_values(own_key, dims, spread, most, cuts=(), kind=jnp.bfloat16):
    entries = jax.random.normal(own_key, dims, jnp.float32) * spread
    if len(cuts) > 0:
        entries = level_of(own_key, dims, cuts, -0.22, 0.18) * entries
    return jnp.clip(entries, min=-most, max=most).astype(kind)


def setup_inputs(seed: int = 0) -> dict:
    splits = jax.random.split(jax.random.key(seed), 7)
    local_weights = normal_values(splits[0], (ISLANDS, LAYERS, KW, D), 1.0, 6.0, ((0, 4), (2, 16), (3, 2)))
    outer_base = normal_values(splits[1], (FRAG, KW, D), 1.0, 6.0, ((1, 16), (2, 2)))
    momentum = normal_values(splits[2], (FRAG, KW, D), 1.0, 6.0, ((1, 16), (2, 2)), jnp.float32)
    layer_order = jax.random.permutation(splits[3], LAYERS).astype(jnp.int32)
    features = normal_values(splits[4], (ISLANDS, TOKENS, D), 1.0, 6.0, ((0, 4), (1, 16), (2, 2)))
    targets = normal_values(splits[5], (ISLANDS, TOKENS, KW), 1.0, 6.0, ((0, 4), (1, 16)))
    return {"local_weights": local_weights, "outer_base": outer_base, "momentum": momentum, "layer_order": layer_order, "features": features, "targets": targets}


outer_mu = 0.9
outer_rate = 0.7
scale_eps = 1e-06

def island_grad(packed):
    weights, layer_idx, tokens_in, target_keys = packed
    key_scale = D ** (-0.5)
    inner_w = lax.dynamic_index_in_dim(weights, layer_idx, 0, keepdims=False)
    keys = jnp.dot(tokens_in, inner_w.T, preferred_element_type=jnp.float32) * key_scale
    residual = (keys - target_keys.astype(jnp.float32)).astype(jnp.bfloat16)
    res_blocks = residual.reshape(N_FSDP, TOK_DEV, KW)
    tok_blocks = tokens_in.reshape(N_FSDP, TOK_DEV, D)

    def add_block(carry, pair):
        res_b, tok_b = pair
        part = (lax.dot_general(res_b, tok_b, (((0,), (0,)), ((), ())), preferred_element_type=jnp.float32) * key_scale).astype(jnp.bfloat16)
        part = lax.optimization_barrier(part)
        return (carry + part.astype(jnp.float32), None)
    summed, _ = lax.scan(add_block, jnp.zeros((KW, D), jnp.float32), (res_blocks, tok_blocks))
    return summed

def reference(local_weights, outer_base, momentum, layer_order, features, targets):
    inner_idx = layer_order[FRAG]
    inner_grad = lax.map(lambda packed: island_grad((packed[0], inner_idx, packed[1], packed[2])), (local_weights, features, targets))
    bases = []
    moments = []
    for slot_index in range(FRAG):
        local_slot = lax.dynamic_index_in_dim(local_weights, layer_order[slot_index], 1, keepdims=False)
        base_slot = outer_base[slot_index].astype(jnp.float32)
        drift = local_slot.astype(jnp.float32) - base_slot[None]
        blocks = drift.reshape(ISLANDS, KW, D // QB, QB)
        block_scale = (lax.optimization_barrier(jnp.max(jnp.abs(blocks), axis=-1)) + scale_eps).astype(jnp.bfloat16)
        quantized = (blocks / block_scale.astype(jnp.float32)[..., None]).astype(jnp.bfloat16)
        quantized = lax.optimization_barrier(quantized)
        restored = quantized.astype(jnp.float32) * block_scale.astype(jnp.float32)[..., None]
        summed = lax.optimization_barrier(jnp.sum(restored, axis=0)).reshape(KW, D)
        mean_drift = summed / ISLANDS
        moment_new = outer_mu * momentum[slot_index] + mean_drift
        base_new = (base_slot + outer_rate * (mean_drift + outer_mu * moment_new)).astype(jnp.bfloat16)
        bases.append(base_new)
        moments.append(moment_new)
    return (jnp.stack(bases), jnp.stack(moments), inner_grad)
```

```python
import jax
import jax.numpy as jnp
from jax import lax
from jax.experimental import pallas as pl
from jax.experimental.pallas import tpu as pltpu
from jax.sharding import PartitionSpec as P

D = 12288
FRAG = 3
QB = 32
KEY_SCALE = D ** (-0.5)

outer_mu = 0.9
outer_rate = 0.7
scale_eps = 1e-06

MESH = pl.DeviceIdType.MESH
BF = jnp.bfloat16
F32 = jnp.float32

HALF = 3072
TT = 256
NT = 2
NCH = 4
QC = 1536
NQ = HALF // QC
NU = NCH * NQ
QT = 512


def nt_dot(a, b):
    return lax.dot_general(a, b, (((1,), (1,)), ((), ())), preferred_element_type=F32)


def kernel(
    lo_ref, lw_hbm, base_hbm, x_hbm, t_hbm,
    og_ref, os_ref,
    lw, base, tt, tpm, xv, wv, wp, ka, kb, kr, ts, tr, rv, gv, r1, r2, sv, nr, uv, pr,
    qo, qs, qr, s2, xr, tot, fr,
    loc_sem, wz_s, wz_r, wp_s, wp_r, wn_s, wn_r, x_s, x_r, kb_s, kb_r, tp_s, tp_r, rr_s, rr_r,
    g_s, g_r, nb_s, nb_r, pr_s, pr_r, q_s, q_r, xl_s, xl_r, fr_s, fr_r,
):
    isl = lax.axis_index("island")
    f = lax.axis_index("fsdp")
    tpi = lax.axis_index("tp")
    core = lax.rem(isl, 2)
    y = lax.div(f, 4)
    z = lax.rem(f, 4)
    yy = lax.rem(y + 3 * core, 4)
    pp = yy + 1 - 2 * lax.rem(yy, 2)
    h = lax.rem(lax.div(yy + 1, 2), 2)
    yp = lax.rem(pp + core, 4)
    yn = lax.rem(3 - yy + core, 4)
    ynp = lax.rem(3 - pp + core, 4)
    yo = [y, yp, yn, ynp]
    zr = lax.rem(z + 1, 4)
    zl = lax.rem(z + 3, 4)
    z2 = lax.rem(z + 2, 4)
    d_pair = {"fsdp": yp * 4 + z}
    d_nb = {"fsdp": yn * 4 + z}
    d_right = {"fsdp": y * 4 + zr}
    d_left = {"fsdp": y * 4 + zl}
    d_tp = {"tp": 1 - tpi}
    d_core = {"island": isl + 1 - 2 * core}
    d_xlo = {"island": lax.rem(isl + 2, 4)}

    mine = pl.ds(pl.multiple_of(h * HALF, HALF), HALF)
    other = pl.ds(pl.multiple_of((1 - h) * HALF, HALF), HALF)

    cp_lw = pltpu.make_async_copy(lw_hbm, lw, loc_sem.at[0])
    cp_lw.start()
    cp_base = pltpu.make_async_copy(base_hbm, base, loc_sem.at[1])
    cp_base.start()
    cp_x = pltpu.make_async_copy(x_hbm.at[:, mine], xv.at[0], loc_sem.at[2])
    cp_x.start()
    cp_t = pltpu.make_async_copy(t_hbm, tt, loc_sem.at[3])
    cp_t.start()

    barrier = pltpu.get_barrier_semaphore()
    for dev in (d_pair, d_nb, d_right, d_left, d_tp, d_core, d_xlo):
        pl.semaphore_signal(barrier, inc=1, device_id=dev, device_id_type=MESH)
    pl.semaphore_wait(barrier, 7)

    started = []

    def copy(src, dst, ss, rs, dev):
        return pltpu.make_async_remote_copy(
            src_ref=src, dst_ref=dst, send_sem=ss, recv_sem=rs, device_id=dev, device_id_type=MESH
        )

    def send(src, dst, ss, rs, dev):
        c = copy(src, dst, ss, rs, dev)
        c.start()
        started.append(c)

    def wait_recv(dst, ss, rs, dev):
        copy(dst, dst, ss, rs, dev).wait_recv()

    def wslot(zo, p, lo, n):
        return wv.at[zo * 4 + yo[p], pl.ds(lo, n)]

    def w_zsend(p, r):
        piece = wslot(z, p, r * 32, 32)
        send(piece, piece, wz_s.at[r, p, 0], wz_r.at[r, p, 0], d_right)
        send(piece, piece, wz_s.at[r, p, 1], wz_r.at[r, p, 1], d_left)

    def w_fwd(p, r):
        wait_recv(wslot(zl, p, r * 32, 32), wz_s.at[r, p, 0], wz_r.at[r, p, 0], d_right)
        a = wslot(zl, p, r * 32, 16)
        send(a, a, wz_s.at[r, p, 2], wz_r.at[r, p, 2], d_right)
        wait_recv(wslot(zr, p, r * 32, 32), wz_s.at[r, p, 1], wz_r.at[r, p, 1], d_left)
        b = wslot(zr, p, r * 32 + 16, 16)
        send(b, b, wz_s.at[r, p, 3], wz_r.at[r, p, 3], d_left)

    def w_end(p, r):
        wait_recv(wslot(z2, p, r * 32, 16), wz_s.at[r, p, 2], wz_r.at[r, p, 2], d_right)
        wait_recv(wslot(z2, p, r * 32 + 16, 16), wz_s.at[r, p, 3], wz_r.at[r, p, 3], d_left)

    def w_pair_send(r):
        send(wp.at[pl.ds(r * 32, 32)], wslot(z, 0, r * 32, 32), wp_s.at[r], wp_r.at[r], d_pair)

    def w_nb_send(p, r):
        piece = wslot(z, p, r * 32, 32)
        send(piece, piece, wn_s.at[p, r], wn_r.at[p, r], d_nb)

    def w_pair_got(r):
        wait_recv(wslot(z, 1, r * 32, 32), wp_s.at[r], wp_r.at[r], d_pair)

    def w_nb_got(p, r):
        wait_recv(wslot(z, 2 + p, r * 32, 32), wn_s.at[p, r], wn_r.at[p, r], d_nb)

    def x_send(t):
        rows = pl.ds(t * TT, TT)
        send(x_hbm.at[rows, other], xv.at[1, rows], x_s.at[t], x_r.at[t], d_pair)

    def x_got(t):
        wait_recv(xv.at[1, pl.ds(t * TT, TT)], x_s.at[t], x_r.at[t], d_pair)

    def chunk_w(c):
        return wv[:, pl.ds(c * 16, 16), :].reshape(256, HALF)

    def key_own(c):
        for t in range(NT):
            ka[c, t] = nt_dot(chunk_w(c), xv[0, pl.ds(t * TT, TT), :])

    def key_pair(c, t):
        kb[c, t] = nt_dot(chunk_w(c), xv[1, pl.ds(t * TT, TT), :]).astype(BF)
        send(kb.at[c, t], kr.at[c, t], kb_s.at[c, t], kb_r.at[c, t], d_pair)

    def key_mid(c, t):
        wait_recv(kr.at[c, t], kb_s.at[c, t], kb_r.at[c, t], d_pair)
        k = ka[c, t] + kr[c, t].astype(F32)
        ka[c, t] = k
        ts[c, t] = k.astype(BF)
        send(ts.at[c, t], tr.at[c, t], tp_s.at[c, t], tp_r.at[c, t], d_tp)

    def key_res(c, t):
        wait_recv(tr.at[c, t], tp_s.at[c, t], tp_r.at[c, t], d_tp)
        keys = (ka[c, t] + tr[c, t].astype(F32)) * KEY_SCALE
        rv[0, c, t] = (keys - tpm[c, :, t * TT:(t + 1) * TT].astype(F32)).astype(BF)
        send(rv.at[0, c, t], rv.at[1, c, t], rr_s.at[c, t], rr_r.at[c, t], d_pair)

    def key_done(c):
        for t in range(NT):
            wait_recv(rv.at[1, c, t], rr_s.at[c, t], rr_r.at[c, t], d_pair)

    def targets_chunk(c):
        row = lax.broadcasted_iota(jnp.int32, (256, 1024), 0)
        col = lax.broadcasted_iota(jnp.int32, (256, 1024), 1)
        slot = row >> 4
        want = ((slot & 3) * 4 + (slot >> 2)) * 64 + c * 16 + (row & 15)
        pick = jnp.where(col == want, 1.0, 0.0).astype(BF)
        tpm[c] = nt_dot(pick, tt[...]).astype(BF)

    def gpart(zo, lo, n, c, q):
        return gv.at[pl.ds(zo * 4 + lo, n), pl.ds(c * 16, 16), pl.ds(q * QC, QC)]

    def grad_unit(u):
        c, q = u // NQ, u % NQ

        @pl.loop(0, QC // 512)
        def _(n):
            cols = pl.ds(pl.multiple_of(q * QC + n * 512, 512), 512)
            acc = None
            for i in range(2):
                for t in range(NT):
                    part = jnp.dot(
                        rv[i, c, t], xv[i, pl.ds(t * TT, TT), cols], preferred_element_type=F32
                    )
                    acc = part if acc is None else acc + part
            gv[:, pl.ds(c * 16, 16), cols] = (acc * KEY_SCALE).astype(BF).reshape(16, 16, 512)

        send(gpart(z2, 0, 2, c, q), r1.at[0, u], g_s.at[u, 0], g_r.at[u, 0], d_right)
        send(gpart(z2, 2, 2, c, q), r1.at[1, u], g_s.at[u, 1], g_r.at[u, 1], d_left)
        send(gpart(zr, 2, 2, c, q), r2.at[0, u, pl.ds(2, 2)], g_s.at[u, 2], g_r.at[u, 2], d_right)
        send(gpart(zl, 0, 2, c, q), r2.at[1, u, pl.ds(0, 2)], g_s.at[u, 3], g_r.at[u, 3], d_left)

    def grad_fwd(u):
        c, q = u // NQ, u % NQ
        rows, cols = pl.ds(c * 16, 16), pl.ds(q * QC, QC)
        wait_recv(r1.at[0, u], g_s.at[u, 0], g_r.at[u, 0], d_right)
        sl = pl.ds(zr * 4, 2)
        gv[sl, rows, cols] = (gv[sl, rows, cols].astype(F32) + r1[0, u].astype(F32)).astype(BF)
        send(gpart(zr, 0, 2, c, q), r2.at[0, u, pl.ds(0, 2)], g_s.at[u, 4], g_r.at[u, 4], d_right)
        wait_recv(r1.at[1, u], g_s.at[u, 1], g_r.at[u, 1], d_left)
        sl2 = pl.ds(zl * 4 + 2, 2)
        gv[sl2, rows, cols] = (gv[sl2, rows, cols].astype(F32) + r1[1, u].astype(F32)).astype(BF)
        send(gpart(zl, 2, 2, c, q), r2.at[1, u, pl.ds(2, 2)], g_s.at[u, 5], g_r.at[u, 5], d_left)

    def grad_ring(u):
        c, q = u // NQ, u % NQ
        wait_recv(r2.at[0, u, pl.ds(2, 2)], g_s.at[u, 2], g_r.at[u, 2], d_right)
        wait_recv(r2.at[1, u, pl.ds(0, 2)], g_s.at[u, 3], g_r.at[u, 3], d_left)
        wait_recv(r2.at[0, u, pl.ds(0, 2)], g_s.at[u, 4], g_r.at[u, 4], d_right)
        wait_recv(r2.at[1, u, pl.ds(2, 2)], g_s.at[u, 5], g_r.at[u, 5], d_left)
        own = gv[pl.ds(z * 4, 4), pl.ds(c * 16, 16), pl.ds(q * QC, QC)].astype(F32)
        sv[u] = (own + r2[0, u].astype(F32) + r2[1, u].astype(F32)).astype(BF)
        send(sv.at[u, yn], nr.at[u, 0], nb_s.at[u, 0], nb_r.at[u, 0], d_nb)
        send(sv.at[u, ynp], nr.at[u, 1], nb_s.at[u, 1], nb_r.at[u, 1], d_nb)

    def grad_pair(u):
        c, q = u // NQ, u % NQ
        wait_recv(nr.at[u, 1], nb_s.at[u, 1], nb_r.at[u, 1], d_nb)
        uv[u] = (sv[u, yp].astype(F32) + nr[u, 1].astype(F32)).astype(BF)
        send(uv.at[u], pr.at[u], pr_s.at[u], pr_r.at[u], d_pair)
        wait_recv(nr.at[u, 0], nb_s.at[u, 0], nb_r.at[u, 0], d_nb)
        cols = pl.ds(pl.multiple_of(h * HALF + q * QC, QC), QC)
        og_ref[c * 16:(c + 1) * 16, cols] = (sv[u, y].astype(F32) + nr[u, 0].astype(F32)).astype(BF)

    def grad_out(u):
        c, q = u // NQ, u % NQ
        wait_recv(pr.at[u], pr_s.at[u], pr_r.at[u], d_pair)
        cols = pl.ds(pl.multiple_of((1 - h) * HALF + q * QC, QC), QC)
        og_ref[c * 16:(c + 1) * 16, cols] = pr[u]

    sel_r = lax.broadcasted_iota(jnp.int32, (128, 128), 0)
    sel_c = lax.broadcasted_iota(jnp.int32, (128, 128), 1)

    def quantize(fi):
        layer = lo_ref[fi]

        def half_of(side, dst):
            @pl.loop(0, HALF // QT)
            def _(j):
                pick = jnp.where(sel_r == (sel_c | (QB - 1)), 1.0, 0.0).astype(BF)
                for k in range(QT // 128):
                    col = pl.multiple_of(side * HALF + j * QT + k * 128, 128)
                    a = lw[layer, :, pl.ds(col, 128)].astype(F32)
                    b = base[fi, :, pl.ds(col, 128)].astype(F32)
                    drift = a - b
                    m = jnp.abs(drift)
                    for s in (1, 2, 4, 8, 16):
                        m = jnp.maximum(m, pltpu.roll(m, s, 1))
                    sc = jnp.dot((m + scale_eps).astype(BF), pick, preferred_element_type=F32)
                    quant = (drift / sc).astype(BF).astype(F32)
                    out = pl.multiple_of(j * QT + k * 128, 128)
                    dst[fi, :, pl.ds(out, 128)] = (quant * sc).astype(BF)

        half_of(1 - core, qs)
        send(qs.at[fi], qr.at[fi], q_s.at[fi], q_r.at[fi], d_core)
        half_of(core, qo)

    def tiles(body):
        @pl.loop(0, HALF // QT)
        def _(j):
            body(pl.ds(pl.multiple_of(j * QT, QT), QT), j)

    def outer_core(fi):
        wait_recv(qr.at[fi], q_s.at[fi], q_r.at[fi], d_core)

        def body(cols, j):
            s2[fi, :, cols] = (qo[fi, :, cols].astype(F32) + qr[fi, :, cols].astype(F32)).astype(BF)

        tiles(body)
        send(s2.at[fi], xr.at[fi], xl_s.at[fi], xl_r.at[fi], d_xlo)

    def outer_x(fi):
        wait_recv(xr.at[fi], xl_s.at[fi], xl_r.at[fi], d_xlo)

        def body(cols, j):
            v = (s2[fi, :, cols].astype(F32) + xr[fi, :, cols].astype(F32)).astype(BF)
            tot[fi, :, cols] = v
            os_ref[fi, :, pl.ds(pl.multiple_of(core * HALF + j * QT, QT), QT)] = v

        tiles(body)
        send(tot.at[fi], fr.at[fi], fr_s.at[fi], fr_r.at[fi], d_core)

    def outer_end(fi):
        wait_recv(fr.at[fi], fr_s.at[fi], fr_r.at[fi], d_core)

        def body(cols, j):
            os_ref[fi, :, pl.ds(pl.multiple_of((1 - core) * HALF + j * QT, QT), QT)] = fr[fi, :, cols]

        tiles(body)

    cp_lw.wait()
    inner = lo_ref[FRAG]
    wv[z * 4 + y] = lw[inner, :, mine]
    wp[...] = lw[inner, :, other]
    for r in range(2):
        w_pair_send(r)
        w_nb_send(0, r)
    for r in range(2):
        w_zsend(0, r)
    for t in range(NT):
        x_send(t)
    cp_base.wait()
    quantize(0)
    w_pair_got(0)
    w_nb_send(1, 0)
    w_zsend(1, 0)
    w_nb_got(0, 0)
    w_zsend(2, 0)
    w_pair_got(1)
    w_nb_send(1, 1)
    w_fwd(0, 0)
    quantize(1)
    w_zsend(1, 1)
    w_nb_got(1, 0)
    w_zsend(3, 0)
    w_nb_got(0, 1)
    w_zsend(2, 1)
    w_fwd(0, 1)
    quantize(2)
    w_nb_got(1, 1)
    w_zsend(3, 1)
    w_fwd(1, 0)
    w_fwd(2, 0)
    for fi in range(FRAG):
        outer_core(fi)
    cp_t.wait()
    for c in range(NCH):
        targets_chunk(c)
    w_fwd(3, 0)
    w_fwd(1, 1)
    for p in range(4):
        w_end(p, 0)
    cp_x.wait()
    key_own(0)
    key_own(1)
    w_fwd(2, 1)
    x_got(0)
    key_pair(0, 0)
    key_pair(1, 0)
    w_fwd(3, 1)
    key_mid(0, 0)
    x_got(1)
    key_pair(0, 1)
    key_pair(1, 1)
    key_mid(1, 0)
    key_mid(0, 1)
    for p in range(4):
        w_end(p, 1)
    key_res(0, 0)
    key_pair(2, 0)
    key_pair(2, 1)
    key_mid(1, 1)
    key_own(2)
    key_res(0, 1)
    key_pair(3, 0)
    key_pair(3, 1)
    key_own(3)
    key_done(0)
    grad_unit(0)
    grad_unit(1)
    key_mid(2, 0)
    key_mid(2, 1)
    key_res(1, 0)
    key_res(1, 1)
    key_mid(3, 0)
    key_mid(3, 1)
    grad_fwd(0)
    key_done(1)
    grad_unit(2)
    grad_fwd(1)
    grad_ring(0)
    grad_unit(3)
    for fi in range(FRAG):
        outer_x(fi)
    key_res(2, 0)
    key_res(2, 1)
    grad_fwd(2)
    grad_ring(1)
    grad_pair(0)
    key_done(2)
    grad_unit(4)
    grad_fwd(3)
    grad_ring(2)
    grad_pair(1)
    grad_out(0)
    grad_unit(5)
    key_res(3, 0)
    key_res(3, 1)
    for fi in range(FRAG):
        outer_end(fi)
    grad_fwd(4)
    key_done(3)
    grad_unit(6)
    grad_ring(3)
    grad_pair(2)
    grad_out(1)
    grad_fwd(5)
    grad_unit(7)
    grad_ring(4)
    grad_pair(3)
    grad_out(2)
    grad_fwd(6)
    grad_ring(5)
    grad_pair(4)
    grad_out(3)
    grad_fwd(7)
    grad_ring(6)
    grad_pair(5)
    grad_out(4)
    grad_ring(7)
    grad_pair(6)
    grad_out(5)
    grad_pair(7)
    grad_out(6)
    grad_out(7)
    for c in started:
        c.wait_send()


def exchange(layer_order, own_layers, outer_base, tokens_in, target_keys):
    vm = pltpu.VMEM
    dma = pltpu.SemaphoreType.DMA
    anyspec = pl.BlockSpec(memory_space=pl.ANY)
    return pl.pallas_call(
        kernel,
        out_shape=(
            jax.ShapeDtypeStruct((64, 2 * HALF), BF),
            jax.ShapeDtypeStruct((FRAG, 64, 2 * HALF), BF),
        ),
        in_specs=[pl.BlockSpec(memory_space=pltpu.SMEM)] + [anyspec] * 4,
        out_specs=(pl.BlockSpec(memory_space=pltpu.VMEM), pl.BlockSpec(memory_space=pltpu.VMEM)),
        scratch_shapes=[
            vm((4, 64, 2 * HALF), BF),
            vm((FRAG, 64, 2 * HALF), BF),
            vm((512, 1024), BF),
            vm((NCH, 256, 512), BF),
            vm((2, 512, HALF), BF),
            vm((16, 64, HALF), BF),
            vm((64, HALF), BF),
            vm((NCH, NT, 256, TT), F32),
            vm((NCH, NT, 256, TT), BF),
            vm((NCH, NT, 256, TT), BF),
            vm((NCH, NT, 256, TT), BF),
            vm((NCH, NT, 256, TT), BF),
            vm((2, NCH, NT, 256, TT), BF),
            vm((16, 64, HALF), BF),
            vm((2, NU, 2, 16, QC), BF),
            vm((2, NU, 4, 16, QC), BF),
            vm((NU, 4, 16, QC), BF),
            vm((NU, 2, 16, QC), BF),
            vm((NU, 16, QC), BF),
            vm((NU, 16, QC), BF),
        ]
        + [vm((FRAG, 64, HALF), BF) for _ in range(7)]
        + [
            dma((4,)),
            dma((2, 4, 4)), dma((2, 4, 4)),
            dma((2,)), dma((2,)),
            dma((2, 2)), dma((2, 2)),
            dma((NT,)), dma((NT,)),
            dma((NCH, NT)), dma((NCH, NT)),
            dma((NCH, NT)), dma((NCH, NT)),
            dma((NCH, NT)), dma((NCH, NT)),
            dma((NU, 6)), dma((NU, 6)),
            dma((NU, 2)), dma((NU, 2)),
            dma((NU,)), dma((NU,)),
            dma((FRAG,)), dma((FRAG,)),
            dma((FRAG,)), dma((FRAG,)),
            dma((FRAG,)), dma((FRAG,)),
        ],
        compiler_params=pltpu.CompilerParams(
            collective_id=0, has_side_effects=True, vmem_limit_bytes=62 * 2**20
        ),
    )(layer_order, own_layers, outer_base, tokens_in, target_keys)


def per_device(local_weights, outer_base, momentum, layer_order, features, targets):
    grad, summed = exchange(layer_order, local_weights[0], outer_base, features[0], targets[0])
    mean_drift = summed.astype(F32) / lax.axis_size("island")
    moment_new = outer_mu * momentum + mean_drift
    base_new = (
        outer_base.astype(F32) + outer_rate * (mean_drift + outer_mu * moment_new)
    ).astype(BF)
    return (base_new, moment_new, grad.astype(F32)[None])


def solution(mesh):
    return jax.shard_map(
        per_device,
        mesh=mesh,
        in_specs=(
            P("island", None, "fsdp", "tp"),
            P(None, "fsdp", "tp"),
            P(None, "fsdp", "tp"),
            P(),
            P("island", "fsdp", "tp"),
            P("island", "fsdp", None),
        ),
        out_specs=(P(None, "fsdp", "tp"), P(None, "fsdp", "tp"), P("island", "fsdp", "tp")),
        check_vma=False,
    )
```

```python
import jax
import jax.numpy as jnp
from jax import lax
from jax.experimental import pallas as pl
from jax.experimental.pallas import tpu as pltpu
from jax.sharding import PartitionSpec as P

D = 12288
FRAG = 3
QB = 32
KEY_SCALE = D ** (-0.5)

outer_mu = 0.9
outer_rate = 0.7
scale_eps = 1e-06

MESH = pl.DeviceIdType.MESH
BF = jnp.bfloat16
F32 = jnp.float32

HALF = 3072
TT = 256
NT = 2
NCH = 4
QC = 1536
NQ = HALF // QC
NU = NCH * NQ
NY = 3
QT = 512


def nt_dot(a, b):
    return lax.dot_general(a, b, (((1,), (1,)), ((), ())), preferred_element_type=F32)


def kernel(
    lo_ref, lw_hbm, base_hbm, x_hbm, t_hbm,
    og_ref, os_hbm,
    lw, base, tt, tpm, xv, wv, wp, ka, kb, kr, ts, tr, rv, gv, r1, r2, sv, nr, uv, pr, yb,
    qo, qs, qr, s2, xr, tot, fr,
    loc_sem, os_sem, step_sem, wz_s, wz_r, wp_s, wp_r, wn_s, wn_r, x_s, x_r, kb_s, kb_r, tp_s, tp_r, rr_s, rr_r,
    g_s, g_r, nb_s, nb_r, yb_s, yb_r, pr_s, pr_r, q_s, q_r, xl_s, xl_r, fr_s, fr_r,
):
    isl = lax.axis_index("island")
    f = lax.axis_index("fsdp")
    tpi = lax.axis_index("tp")
    core = lax.rem(isl, 2)
    y = lax.div(f, 4)
    z = lax.rem(f, 4)
    yy = lax.rem(y + 3 * core, 4)
    pp = yy + 1 - 2 * lax.rem(yy, 2)
    h = lax.rem(lax.div(yy + 1, 2), 2)
    yp = lax.rem(pp + core, 4)
    yn = lax.rem(3 - yy + core, 4)
    e = lax.rem(yy, 2)
    slot_of = [e, 1 - e, 3 - e, 2 + e]
    base_y = 2 * lax.div(yy, 2)
    slot_y = [lax.rem(v + core, 4) for v in (base_y, base_y + 1, 2 - base_y, 3 - base_y)]
    zr = lax.rem(z + 1, 4)
    zl = lax.rem(z + 3, 4)
    z2 = lax.rem(z + 2, 4)
    d_pair = {"fsdp": yp * 4 + z}
    d_nb = {"fsdp": yn * 4 + z}
    d_right = {"fsdp": y * 4 + zr}
    d_left = {"fsdp": y * 4 + zl}
    d_tp = {"tp": 1 - tpi}
    d_core = {"island": isl + 1 - 2 * core}
    d_xlo = {"island": lax.rem(isl + 2, 4)}

    mine = pl.ds(pl.multiple_of(h * HALF, HALF), HALF)
    other = pl.ds(pl.multiple_of((1 - h) * HALF, HALF), HALF)

    barrier = pltpu.get_barrier_semaphore()
    for dev in (d_pair, d_nb, d_right, d_left, d_tp, d_core, d_xlo):
        pl.semaphore_signal(barrier, inc=1, device_id=dev, device_id_type=MESH)

    cp_lw = pltpu.make_async_copy(lw_hbm, lw, loc_sem.at[0])
    cp_lw.start()
    cp_base = pltpu.make_async_copy(base_hbm, base, loc_sem.at[1])
    cp_base.start()
    cp_x = pltpu.make_async_copy(x_hbm.at[:, mine], xv.at[0], loc_sem.at[2])
    cp_x.start()
    cp_t = pltpu.make_async_copy(t_hbm, tt, loc_sem.at[3])
    cp_t.start()

    cp_lw.wait()
    inner = lo_ref[FRAG]
    wv[z, e] = lw[inner, :, mine]
    wp[...] = lw[inner, :, other]
    pl.semaphore_wait(barrier, 7)

    started = []

    def copy(src, dst, ss, rs, dev):
        return pltpu.make_async_remote_copy(
            src_ref=src, dst_ref=dst, send_sem=ss, recv_sem=rs, device_id=dev, device_id_type=MESH
        )

    def send(src, dst, ss, rs, dev):
        c = copy(src, dst, ss, rs, dev)
        c.start()
        started.append(c)

    def wait_recv(dst, ss, rs, dev):
        copy(dst, dst, ss, rs, dev).wait_recv()

    def wslot(zo, p, lo, n):
        return wv.at[zo, slot_of[p], pl.ds(lo, n)]

    def w_zsend(p, r):
        piece = wslot(z, p, r * 32, 32)
        send(piece, piece, wz_s.at[r, p, 0], wz_r.at[r, p, 0], d_right)
        send(piece, piece, wz_s.at[r, p, 1], wz_r.at[r, p, 1], d_left)

    def w_fwd(p, r):
        wait_recv(wslot(zl, p, r * 32, 32), wz_s.at[r, p, 0], wz_r.at[r, p, 0], d_right)
        a = wslot(zl, p, r * 32, 16)
        send(a, a, wz_s.at[r, p, 2], wz_r.at[r, p, 2], d_right)
        wait_recv(wslot(zr, p, r * 32, 32), wz_s.at[r, p, 1], wz_r.at[r, p, 1], d_left)
        b = wslot(zr, p, r * 32 + 16, 16)
        send(b, b, wz_s.at[r, p, 3], wz_r.at[r, p, 3], d_left)

    def w_end(p, r):
        wait_recv(wslot(z2, p, r * 32, 16), wz_s.at[r, p, 2], wz_r.at[r, p, 2], d_right)
        wait_recv(wslot(z2, p, r * 32 + 16, 16), wz_s.at[r, p, 3], wz_r.at[r, p, 3], d_left)

    def w_pair_send(r):
        send(wp.at[pl.ds(r * 32, 32)], wslot(z, 0, r * 32, 32), wp_s.at[r], wp_r.at[r], d_pair)

    def w_nb_send(p, r):
        piece = wslot(z, p, r * 32, 32)
        there = wv.at[z, 2 + slot_of[p], pl.ds(r * 32, 32)]
        send(piece, there, wn_s.at[p, r], wn_r.at[p, r], d_nb)

    def w_pair_got(r):
        wait_recv(wslot(z, 1, r * 32, 32), wp_s.at[r], wp_r.at[r], d_pair)

    def w_nb_got(p, r):
        wait_recv(wslot(z, 2 + p, r * 32, 32), wn_s.at[p, r], wn_r.at[p, r], d_nb)

    def x_send(t):
        rows = pl.ds(t * TT, TT)
        send(x_hbm.at[rows, other], xv.at[1, rows], x_s.at[t], x_r.at[t], d_pair)

    def x_got(t):
        wait_recv(xv.at[1, pl.ds(t * TT, TT)], x_s.at[t], x_r.at[t], d_pair)

    def chunk_w(c):
        return wv[:, :, pl.ds(c * 16, 16), :].reshape(256, HALF)

    def key_own(c):
        for t in range(NT):
            ka[c, t] = nt_dot(chunk_w(c), xv[0, pl.ds(t * TT, TT), :])

    def key_pair(c, t):
        kb[c, t] = nt_dot(chunk_w(c), xv[1, pl.ds(t * TT, TT), :]).astype(BF)
        send(kb.at[c, t], kr.at[c, t], kb_s.at[c, t], kb_r.at[c, t], d_pair)

    def key_mid(c, t):
        wait_recv(kr.at[c, t], kb_s.at[c, t], kb_r.at[c, t], d_pair)
        k = ka[c, t] + kr[c, t].astype(F32)
        ka[c, t] = k
        ts[c, t] = k.astype(BF)
        send(ts.at[c, t], tr.at[c, t], tp_s.at[c, t], tp_r.at[c, t], d_tp)

    def key_res(c, t):
        wait_recv(tr.at[c, t], tp_s.at[c, t], tp_r.at[c, t], d_tp)
        keys = (ka[c, t] + tr[c, t].astype(F32)) * KEY_SCALE
        rv[0, c, t] = (keys - tpm[c, :, t * TT:(t + 1) * TT].astype(F32)).astype(BF)
        send(rv.at[0, c, t], rv.at[1, c, t], rr_s.at[c, t], rr_r.at[c, t], d_pair)

    def key_done(c):
        for t in range(NT):
            wait_recv(rv.at[1, c, t], rr_s.at[c, t], rr_r.at[c, t], d_pair)

    def targets_chunk(c):
        row = lax.broadcasted_iota(jnp.int32, (256, 1024), 0)
        col = lax.broadcasted_iota(jnp.int32, (256, 1024), 1)
        slot = row >> 4
        p = slot & 3
        owner_y = jnp.where(p < 2, jnp.where(p == 0, slot_y[0], slot_y[1]), jnp.where(p == 2, slot_y[2], slot_y[3]))
        want = (owner_y * 4 + (slot >> 2)) * 64 + c * 16 + (row & 15)
        pick = jnp.where(col == want, 1.0, 0.0).astype(BF)
        tpm[c] = nt_dot(pick, tt[...]).astype(BF)

    def gcut(zo, lo, n, u):
        c, q = u // NQ, u % NQ
        return zo, pl.ds(lo, n), pl.ds(c * 16, 16), pl.ds(q * QC, QC)

    def late(u):
        return u >= NU - NY

    def grad_unit(u):
        c, q = u // NQ, u % NQ

        @pl.loop(0, QC // 512)
        def _(n):
            cols = pl.ds(pl.multiple_of(q * QC + n * 512, 512), 512)
            acc = None
            for i in range(2):
                for t in range(NT):
                    part = jnp.dot(
                        rv[i, c, t], xv[i, pl.ds(t * TT, TT), cols], preferred_element_type=F32
                    )
                    acc = part if acc is None else acc + part
            gv[:, :, pl.ds(c * 16, 16), cols] = (acc * KEY_SCALE).astype(BF).reshape(4, 4, 16, 512)

        if late(u):
            src = gv.at[:, pl.ds(2, 2), pl.ds(c * 16, 16), pl.ds(q * QC, QC)]
            v = u - (NU - NY)
            send(src, yb.at[v], yb_s.at[v], yb_r.at[v], d_nb)
        else:
            grad_start(u, 2)

    def grad_start(u, n):
        lo, hi = pl.ds(0, n), pl.ds(n, n)
        send(gv.at[gcut(z2, 0, n, u)], r1.at[0, u, lo], g_s.at[u, 0], g_r.at[u, 0], d_right)
        send(gv.at[gcut(z2, n, n, u)], r1.at[1, u, lo], g_s.at[u, 1], g_r.at[u, 1], d_left)
        send(gv.at[gcut(zr, n, n, u)], r2.at[0, u, hi], g_s.at[u, 2], g_r.at[u, 2], d_right)
        send(gv.at[gcut(zl, 0, n, u)], r2.at[1, u, lo], g_s.at[u, 3], g_r.at[u, 3], d_left)

    def grad_nb(u):
        if not late(u):
            return
        c, q = u // NQ, u % NQ
        v = u - (NU - NY)
        wait_recv(yb.at[v], yb_s.at[v], yb_r.at[v], d_nb)
        for zo in range(4):
            cut = gcut(zo, 0, 2, u)
            gv[cut] = (gv[cut].astype(F32) + yb[v, zo].astype(F32)).astype(BF)
        grad_start(u, 1)

    def grad_fwd(u):
        n = 1 if late(u) else 2
        lo, hi = pl.ds(0, n), pl.ds(n, n)
        wait_recv(r1.at[0, u, lo], g_s.at[u, 0], g_r.at[u, 0], d_right)
        cut = gcut(zr, 0, n, u)
        gv[cut] = (gv[cut].astype(F32) + r1[0, u, 0:n].astype(F32)).astype(BF)
        send(gv.at[cut], r2.at[0, u, lo], g_s.at[u, 4], g_r.at[u, 4], d_right)
        wait_recv(r1.at[1, u, lo], g_s.at[u, 1], g_r.at[u, 1], d_left)
        cut = gcut(zl, n, n, u)
        gv[cut] = (gv[cut].astype(F32) + r1[1, u, 0:n].astype(F32)).astype(BF)
        send(gv.at[cut], r2.at[1, u, hi], g_s.at[u, 5], g_r.at[u, 5], d_left)

    def grad_ring(u):
        n = 1 if late(u) else 2
        lo, hi = pl.ds(0, n), pl.ds(n, n)
        wait_recv(r2.at[0, u, hi], g_s.at[u, 2], g_r.at[u, 2], d_right)
        wait_recv(r2.at[1, u, lo], g_s.at[u, 3], g_r.at[u, 3], d_left)
        wait_recv(r2.at[0, u, lo], g_s.at[u, 4], g_r.at[u, 4], d_right)
        wait_recv(r2.at[1, u, hi], g_s.at[u, 5], g_r.at[u, 5], d_left)
        own = gv[gcut(z, 0, 2 * n, u)].astype(F32)
        own = own + r2[0, u, 0:2 * n].astype(F32) + r2[1, u, 0:2 * n].astype(F32)
        if late(u):
            sv[u, 0:2] = own.astype(BF)
            send(sv.at[u, 1 - e], pr.at[u], pr_s.at[u], pr_r.at[u], d_pair)
            grad_store(u, h, sv[u, e])
        else:
            sv[u] = own.astype(BF)
            send(sv.at[u, pl.ds(2, 2)], nr.at[u], nb_s.at[u], nb_r.at[u], d_nb)

    def grad_store(u, side, value):
        c, q = u // NQ, u % NQ
        cols = pl.ds(pl.multiple_of(side * HALF + q * QC, QC), QC)
        og_ref[c * 16:(c + 1) * 16, cols] = value

    def grad_pair(u):
        if late(u):
            return
        wait_recv(nr.at[u], nb_s.at[u], nb_r.at[u], d_nb)
        uv[u] = (sv[u, 1 - e].astype(F32) + nr[u, 1 - e].astype(F32)).astype(BF)
        send(uv.at[u], pr.at[u], pr_s.at[u], pr_r.at[u], d_pair)
        grad_store(u, h, (sv[u, e].astype(F32) + nr[u, e].astype(F32)).astype(BF))

    def grad_out(u):
        wait_recv(pr.at[u], pr_s.at[u], pr_r.at[u], d_pair)
        grad_store(u, 1 - h, pr[u])

    sel_r = lax.broadcasted_iota(jnp.int32, (128, 128), 0)
    sel_c = lax.broadcasted_iota(jnp.int32, (128, 128), 1)

    def quantize(fi, own):
        layer = lo_ref[fi]
        side, dst = (core, qo) if own else (1 - core, qs)

        @pl.loop(0, HALF // QT)
        def _(j):
            pick = jnp.where(sel_r == (sel_c | (QB - 1)), 1.0, 0.0).astype(BF)
            for k in range(QT // 128):
                col = pl.multiple_of(side * HALF + j * QT + k * 128, 128)
                a = lw[layer, :, pl.ds(col, 128)].astype(F32)
                b = base[fi, :, pl.ds(col, 128)].astype(F32)
                drift = a - b
                m = jnp.abs(drift)
                for s in (1, 2, 4, 8, 16):
                    m = jnp.maximum(m, pltpu.roll(m, s, 1))
                sc = jnp.dot((m + scale_eps).astype(BF), pick, preferred_element_type=F32)
                quant = (drift / sc).astype(BF).astype(F32)
                out = pl.multiple_of(j * QT + k * 128, 128)
                dst[fi, :, pl.ds(out, 128)] = (quant * sc).astype(BF)

        if not own:
            send(qs.at[fi], qr.at[fi], q_s.at[fi], q_r.at[fi], d_core)

    def tiles(body):
        @pl.loop(0, HALF // QT)
        def _(j):
            body(pl.ds(pl.multiple_of(j * QT, QT), QT), j)

    def outer_core(fi):
        wait_recv(qr.at[fi], q_s.at[fi], q_r.at[fi], d_core)

        def body(cols, j):
            s2[fi, :, cols] = (qo[fi, :, cols].astype(F32) + qr[fi, :, cols].astype(F32)).astype(BF)

        tiles(body)
        send(s2.at[fi], xr.at[fi], xl_s.at[fi], xl_r.at[fi], d_xlo)

    def outer_x(fi):
        wait_recv(xr.at[fi], xl_s.at[fi], xl_r.at[fi], d_xlo)

        def body(cols, j):
            tot[fi, :, cols] = (s2[fi, :, cols].astype(F32) + xr[fi, :, cols].astype(F32)).astype(BF)

        tiles(body)
        send(tot.at[fi], fr.at[fi], fr_s.at[fi], fr_r.at[fi], d_core)
        write_sum(tot, fi, core, 0)

    def write_sum(src, fi, side, k):
        cols = pl.ds(pl.multiple_of(side * HALF, HALF), HALF)
        c = pltpu.make_async_copy(src.at[fi], os_hbm.at[fi, :, cols], os_sem.at[fi, k])
        c.start()
        written.append(c)

    def outer_end(fi):
        wait_recv(fr.at[fi], fr_s.at[fi], fr_r.at[fi], d_core)
        write_sum(fr, fi, 1 - core, 1)

    written = []

    def in_step():
        pl.semaphore_signal(step_sem, inc=1, device_id=d_core, device_id_type=MESH)
        pl.semaphore_wait(step_sem, 1)

    for r in range(2):
        w_pair_send(r)
        w_nb_send(0, r)
    for r in range(2):
        w_zsend(0, r)
    for t in range(NT):
        x_send(t)
    cp_base.wait()
    quantize(0, False)
    quantize(0, True)
    w_pair_got(0)
    w_nb_send(1, 0)
    w_zsend(1, 0)
    w_nb_got(0, 0)
    w_zsend(2, 0)
    w_pair_got(1)
    w_nb_send(1, 1)
    w_fwd(0, 0)
    quantize(1, False)
    quantize(1, True)
    w_zsend(1, 1)
    w_nb_got(1, 0)
    w_zsend(3, 0)
    w_nb_got(0, 1)
    w_zsend(2, 1)
    w_fwd(0, 1)
    quantize(2, False)
    quantize(2, True)
    w_nb_got(1, 1)
    w_zsend(3, 1)
    w_fwd(1, 0)
    w_fwd(2, 0)
    for fi in range(FRAG):
        outer_core(fi)
    cp_t.wait()
    for c in range(NCH):
        targets_chunk(c)
    w_fwd(3, 0)
    w_fwd(1, 1)
    for p in range(4):
        w_end(p, 0)
    cp_x.wait()
    key_own(0)
    key_own(1)
    w_fwd(2, 1)
    x_got(0)
    key_pair(0, 0)
    key_pair(1, 0)
    w_fwd(3, 1)
    key_mid(0, 0)
    x_got(1)
    key_pair(0, 1)
    key_pair(1, 1)
    key_mid(1, 0)
    key_mid(0, 1)
    for p in range(4):
        w_end(p, 1)
    key_res(0, 0)
    key_pair(2, 0)
    key_pair(2, 1)
    key_mid(1, 1)
    key_own(2)
    key_res(0, 1)
    key_pair(3, 0)
    key_pair(3, 1)
    key_own(3)
    key_done(0)
    in_step()
    grad_unit(0)
    key_mid(2, 0)
    key_mid(2, 1)
    key_res(1, 0)
    key_res(1, 1)
    in_step()
    grad_unit(1)
    key_mid(3, 0)
    key_mid(3, 1)
    grad_fwd(0)
    key_done(1)
    in_step()
    grad_unit(2)
    key_res(2, 0)
    key_res(2, 1)
    grad_fwd(1)
    grad_ring(0)
    outer_x(0)
    key_res(3, 0)
    key_res(3, 1)
    in_step()
    grad_unit(3)
    key_done(2)
    grad_fwd(2)
    grad_ring(1)
    grad_pair(0)
    in_step()
    grad_unit(5)
    grad_unit(4)
    outer_x(1)
    key_done(3)
    grad_fwd(3)
    grad_ring(2)
    grad_pair(1)
    grad_out(0)
    in_step()
    grad_unit(6)
    grad_unit(7)
    outer_x(2)
    grad_nb(5)
    grad_fwd(4)
    grad_ring(3)
    grad_pair(2)
    grad_out(1)
    in_step()
    grad_nb(6)
    grad_fwd(5)
    grad_ring(4)
    grad_pair(3)
    grad_out(2)
    for fi in range(FRAG):
        outer_end(fi)
    in_step()
    grad_nb(7)
    grad_fwd(6)
    grad_ring(5)
    grad_pair(4)
    grad_out(3)
    grad_fwd(7)
    grad_ring(6)
    grad_out(4)
    grad_out(5)
    grad_ring(7)
    grad_out(6)
    grad_out(7)
    for c in written:
        c.wait()
    for c in started:
        c.wait_send()


def exchange(layer_order, own_layers, outer_base, tokens_in, target_keys):
    vm = pltpu.VMEM
    dma = pltpu.SemaphoreType.DMA
    anyspec = pl.BlockSpec(memory_space=pl.ANY)
    return pl.pallas_call(
        kernel,
        out_shape=(
            jax.ShapeDtypeStruct((64, 2 * HALF), BF),
            jax.ShapeDtypeStruct((FRAG, 64, 2 * HALF), BF),
        ),
        in_specs=[pl.BlockSpec(memory_space=pltpu.SMEM)] + [anyspec] * 4,
        out_specs=(pl.BlockSpec(memory_space=pltpu.VMEM), anyspec),
        scratch_shapes=[
            vm((4, 64, 2 * HALF), BF),
            vm((FRAG, 64, 2 * HALF), BF),
            vm((512, 1024), BF),
            vm((NCH, 256, 512), BF),
            vm((2, 512, HALF), BF),
            vm((4, 4, 64, HALF), BF),
            vm((64, HALF), BF),
            vm((NCH, NT, 256, TT), F32),
            vm((NCH, NT, 256, TT), BF),
            vm((NCH, NT, 256, TT), BF),
            vm((NCH, NT, 256, TT), BF),
            vm((NCH, NT, 256, TT), BF),
            vm((2, NCH, NT, 256, TT), BF),
            vm((4, 4, 64, HALF), BF),
            vm((2, NU, 2, 16, QC), BF),
            vm((2, NU, 4, 16, QC), BF),
            vm((NU, 4, 16, QC), BF),
            vm((NU, 2, 16, QC), BF),
            vm((NU, 16, QC), BF),
            vm((NU, 16, QC), BF),
            vm((NY, 4, 2, 16, QC), BF),
        ]
        + [vm((FRAG, 64, HALF), BF) for _ in range(7)]
        + [
            dma((4,)), dma((FRAG, 2)), pltpu.SemaphoreType.REGULAR,
            dma((2, 4, 4)), dma((2, 4, 4)),
            dma((2,)), dma((2,)),
            dma((2, 2)), dma((2, 2)),
            dma((NT,)), dma((NT,)),
            dma((NCH, NT)), dma((NCH, NT)),
            dma((NCH, NT)), dma((NCH, NT)),
            dma((NCH, NT)), dma((NCH, NT)),
            dma((NU, 6)), dma((NU, 6)),
            dma((NU,)), dma((NU,)),
            dma((NY,)), dma((NY,)),
            dma((NU,)), dma((NU,)),
            dma((FRAG,)), dma((FRAG,)),
            dma((FRAG,)), dma((FRAG,)),
            dma((FRAG,)), dma((FRAG,)),
        ],
        compiler_params=pltpu.CompilerParams(
            collective_id=0, has_side_effects=True, vmem_limit_bytes=62 * 2**20
        ),
    )(layer_order, own_layers, outer_base, tokens_in, target_keys)


def per_device(local_weights, outer_base, momentum, layer_order, features, targets):
    grad, summed = exchange(layer_order, local_weights[0], outer_base, features[0], targets[0])
    mean_drift = summed.astype(F32) / lax.axis_size("island")
    moment_new = outer_mu * momentum + mean_drift
    base_new = (
        outer_base.astype(F32) + outer_rate * (mean_drift + outer_mu * moment_new)
    ).astype(BF)
    return (base_new, moment_new, grad.astype(F32)[None])


def solution(mesh):
    return jax.shard_map(
        per_device,
        mesh=mesh,
        in_specs=(
            P("island", None, "fsdp", "tp"),
            P(None, "fsdp", "tp"),
            P(None, "fsdp", "tp"),
            P(),
            P("island", "fsdp", "tp"),
            P("island", "fsdp", None),
        ),
        out_specs=(P(None, "fsdp", "tp"), P(None, "fsdp", "tp"), P("island", "fsdp", "tp")),
        check_vma=False,
    )
```

```python
import jax
import jax.numpy as jnp
from jax import lax
from jax.experimental import pallas as pl
from jax.experimental.pallas import tpu as pltpu
from jax.sharding import PartitionSpec as P

D = 12288
FRAG = 3
QB = 32
KEY_SCALE = D ** (-0.5)

outer_mu = 0.9
outer_rate = 0.7
scale_eps = 1e-06

MESH = pl.DeviceIdType.MESH
BF = jnp.bfloat16
F32 = jnp.float32

HALF = 3072
TT = 256
NT = 2
NCH = 4
QC = 1536
NQ = HALF // QC
NU = NCH * NQ
NY = 3
QT = 512


def nt_dot(a, b):
    return lax.dot_general(a, b, (((1,), (1,)), ((), ())), preferred_element_type=F32)


def kernel(
    lo_ref, lw_hbm, base_hbm, x_hbm, t_hbm,
    og_ref, os_hbm,
    tt, tpm, xv, wv, wp, ka, kb, kr, ts, tr, rv, gv, r1, r2, sv, nr, uv, pr, yb,
    qo, qs, qr, s2, xr, fr,
    loc_sem, load_sem, os_sem, step_sem, wz_s, wz_r, wp_s, wp_r, wn_s, wn_r, x_s, x_r, kb_s, kb_r, tp_s, tp_r, rr_s, rr_r,
    g_s, g_r, nb_s, nb_r, yb_s, yb_r, pr_s, pr_r, q_s, q_r, xl_s, xl_r, fr_s, fr_r,
):
    isl = lax.axis_index("island")
    f = lax.axis_index("fsdp")
    tpi = lax.axis_index("tp")
    core = lax.rem(isl, 2)
    y = lax.div(f, 4)
    z = lax.rem(f, 4)
    yy = lax.rem(y + 3 * core, 4)
    pp = yy + 1 - 2 * lax.rem(yy, 2)
    h = lax.rem(lax.div(yy + 1, 2), 2)
    yp = lax.rem(pp + core, 4)
    yn = lax.rem(3 - yy + core, 4)
    e = lax.rem(yy, 2)
    slot_of = [e, 1 - e, 3 - e, 2 + e]
    base_y = 2 * lax.div(yy, 2)
    slot_y = [lax.rem(v + core, 4) for v in (base_y, base_y + 1, 2 - base_y, 3 - base_y)]
    zr = lax.rem(z + 1, 4)
    zl = lax.rem(z + 3, 4)
    z2 = lax.rem(z + 2, 4)
    d_pair = {"fsdp": yp * 4 + z}
    d_nb = {"fsdp": yn * 4 + z}
    d_right = {"fsdp": y * 4 + zr}
    d_left = {"fsdp": y * 4 + zl}
    d_tp = {"tp": 1 - tpi}
    d_core = {"island": isl + 1 - 2 * core}
    d_xlo = {"island": lax.rem(isl + 2, 4)}

    mine = pl.ds(pl.multiple_of(h * HALF, HALF), HALF)
    other = pl.ds(pl.multiple_of((1 - h) * HALF, HALF), HALF)

    barrier = pltpu.get_barrier_semaphore()
    for dev in (d_pair, d_nb, d_right, d_left, d_tp, d_core, d_xlo):
        pl.semaphore_signal(barrier, inc=1, device_id=dev, device_id_type=MESH)

    loads = []

    def load(src, n, first, count):
        for layer in range(count):
            for side in range(2):
                cut = src.at[layer, :, pl.ds(side * HALF, HALF)]
                c = pltpu.make_async_copy(cut, gv.at[layer, first + side], load_sem.at[n, layer, side])
                c.start()
                loads.append(c)

    load(lw_hbm, 0, 0, 4)
    cp_x = pltpu.make_async_copy(x_hbm.at[:, mine], xv.at[0], loc_sem.at[2])
    cp_x.start()
    cp_t = pltpu.make_async_copy(t_hbm, tt, loc_sem.at[3])
    cp_t.start()

    for c in loads:
        c.wait()
    inner = lo_ref[FRAG]
    wv[z, e] = gv[inner, h]
    wp[...] = gv[inner, 1 - h]
    load(base_hbm, 1, 2, FRAG)
    pl.semaphore_wait(barrier, 7)

    started = []

    def copy(src, dst, ss, rs, dev):
        return pltpu.make_async_remote_copy(
            src_ref=src, dst_ref=dst, send_sem=ss, recv_sem=rs, device_id=dev, device_id_type=MESH
        )

    def send(src, dst, ss, rs, dev):
        c = copy(src, dst, ss, rs, dev)
        c.start()
        started.append(c)

    def wait_recv(dst, ss, rs, dev):
        copy(dst, dst, ss, rs, dev).wait_recv()

    def wslot(zo, p, lo, n):
        return wv.at[zo, slot_of[p], pl.ds(lo, n)]

    def w_zsend(p, r):
        piece = wslot(z, p, r * 32, 32)
        send(piece, piece, wz_s.at[r, p, 0], wz_r.at[r, p, 0], d_right)
        send(piece, piece, wz_s.at[r, p, 1], wz_r.at[r, p, 1], d_left)

    def w_fwd(p, r):
        wait_recv(wslot(zl, p, r * 32, 32), wz_s.at[r, p, 0], wz_r.at[r, p, 0], d_right)
        a = wslot(zl, p, r * 32, 16)
        send(a, a, wz_s.at[r, p, 2], wz_r.at[r, p, 2], d_right)
        wait_recv(wslot(zr, p, r * 32, 32), wz_s.at[r, p, 1], wz_r.at[r, p, 1], d_left)
        b = wslot(zr, p, r * 32 + 16, 16)
        send(b, b, wz_s.at[r, p, 3], wz_r.at[r, p, 3], d_left)

    def w_end(p, r):
        wait_recv(wslot(z2, p, r * 32, 16), wz_s.at[r, p, 2], wz_r.at[r, p, 2], d_right)
        wait_recv(wslot(z2, p, r * 32 + 16, 16), wz_s.at[r, p, 3], wz_r.at[r, p, 3], d_left)

    def w_pair_send(r):
        send(wp.at[pl.ds(r * 32, 32)], wslot(z, 0, r * 32, 32), wp_s.at[r], wp_r.at[r], d_pair)

    def w_nb_send(p, r):
        piece = wslot(z, p, r * 32, 32)
        there = wv.at[z, 2 + slot_of[p], pl.ds(r * 32, 32)]
        send(piece, there, wn_s.at[p, r], wn_r.at[p, r], d_nb)

    def w_pair_got(r):
        wait_recv(wslot(z, 1, r * 32, 32), wp_s.at[r], wp_r.at[r], d_pair)

    def w_nb_got(p, r):
        wait_recv(wslot(z, 2 + p, r * 32, 32), wn_s.at[p, r], wn_r.at[p, r], d_nb)

    def x_send(t):
        rows = pl.ds(t * TT, TT)
        send(x_hbm.at[rows, other], xv.at[1, rows], x_s.at[t], x_r.at[t], d_pair)

    def x_got(t):
        wait_recv(xv.at[1, pl.ds(t * TT, TT)], x_s.at[t], x_r.at[t], d_pair)

    def chunk_w(c):
        return wv[:, :, pl.ds(c * 16, 16), :].reshape(256, HALF)

    def key_own(c):
        for t in range(NT):
            ka[c, t] = nt_dot(chunk_w(c), xv[0, pl.ds(t * TT, TT), :])

    def key_pair(c, t):
        kb[c, t] = nt_dot(chunk_w(c), xv[1, pl.ds(t * TT, TT), :]).astype(BF)
        send(kb.at[c, t], kr.at[c, t], kb_s.at[c, t], kb_r.at[c, t], d_pair)

    def key_mid(c, t):
        wait_recv(kr.at[c, t], kb_s.at[c, t], kb_r.at[c, t], d_pair)
        k = ka[c, t] + kr[c, t].astype(F32)
        ka[c, t] = k
        ts[c, t] = k.astype(BF)
        send(ts.at[c, t], tr.at[c, t], tp_s.at[c, t], tp_r.at[c, t], d_tp)

    def key_res(c, t):
        wait_recv(tr.at[c, t], tp_s.at[c, t], tp_r.at[c, t], d_tp)
        keys = (ka[c, t] + tr[c, t].astype(F32)) * KEY_SCALE
        rv[0, c, t] = (keys - tpm[c, :, t * TT:(t + 1) * TT].astype(F32)).astype(BF)
        send(rv.at[0, c, t], rv.at[1, c, t], rr_s.at[c, t], rr_r.at[c, t], d_pair)

    def key_done(c):
        for t in range(NT):
            wait_recv(rv.at[1, c, t], rr_s.at[c, t], rr_r.at[c, t], d_pair)

    def targets_chunk(c):
        row = lax.broadcasted_iota(jnp.int32, (256, 1024), 0)
        col = lax.broadcasted_iota(jnp.int32, (256, 1024), 1)
        slot = row >> 4
        p = slot & 3
        owner_y = jnp.where(p < 2, jnp.where(p == 0, slot_y[0], slot_y[1]), jnp.where(p == 2, slot_y[2], slot_y[3]))
        want = (owner_y * 4 + (slot >> 2)) * 64 + c * 16 + (row & 15)
        pick = jnp.where(col == want, 1.0, 0.0).astype(BF)
        tpm[c] = nt_dot(pick, tt[...]).astype(BF)

    def gcut(zo, lo, n, u):
        c, q = u // NQ, u % NQ
        return zo, pl.ds(lo, n), pl.ds(c * 16, 16), pl.ds(q * QC, QC)

    def late(u):
        return u >= NU - NY

    def grad_unit(u):
        c, q = u // NQ, u % NQ

        @pl.loop(0, QC // 512)
        def _(n):
            cols = pl.ds(pl.multiple_of(q * QC + n * 512, 512), 512)
            acc = None
            for i in range(2):
                for t in range(NT):
                    part = jnp.dot(
                        rv[i, c, t], xv[i, pl.ds(t * TT, TT), cols], preferred_element_type=F32
                    )
                    acc = part if acc is None else acc + part
            gv[:, :, pl.ds(c * 16, 16), cols] = (acc * KEY_SCALE).astype(BF).reshape(4, 4, 16, 512)

        if late(u):
            src = gv.at[:, pl.ds(2, 2), pl.ds(c * 16, 16), pl.ds(q * QC, QC)]
            v = u - (NU - NY)
            send(src, yb.at[v], yb_s.at[v], yb_r.at[v], d_nb)
        else:
            grad_start(u, 2)

    def grad_start(u, n):
        lo, hi = pl.ds(0, n), pl.ds(n, n)
        send(gv.at[gcut(z2, 0, n, u)], r1.at[0, u, lo], g_s.at[u, 0], g_r.at[u, 0], d_right)
        send(gv.at[gcut(z2, n, n, u)], r1.at[1, u, lo], g_s.at[u, 1], g_r.at[u, 1], d_left)
        send(gv.at[gcut(zr, n, n, u)], r2.at[0, u, hi], g_s.at[u, 2], g_r.at[u, 2], d_right)
        send(gv.at[gcut(zl, 0, n, u)], r2.at[1, u, lo], g_s.at[u, 3], g_r.at[u, 3], d_left)

    def grad_nb(u):
        if not late(u):
            return
        c, q = u // NQ, u % NQ
        v = u - (NU - NY)
        wait_recv(yb.at[v], yb_s.at[v], yb_r.at[v], d_nb)
        for zo in range(4):
            cut = gcut(zo, 0, 2, u)
            gv[cut] = (gv[cut].astype(F32) + yb[v, zo].astype(F32)).astype(BF)
        grad_start(u, 1)

    def grad_fwd(u):
        n = 1 if late(u) else 2
        lo, hi = pl.ds(0, n), pl.ds(n, n)
        wait_recv(r1.at[0, u, lo], g_s.at[u, 0], g_r.at[u, 0], d_right)
        cut = gcut(zr, 0, n, u)
        gv[cut] = (gv[cut].astype(F32) + r1[0, u, 0:n].astype(F32)).astype(BF)
        send(gv.at[cut], r2.at[0, u, lo], g_s.at[u, 4], g_r.at[u, 4], d_right)
        wait_recv(r1.at[1, u, lo], g_s.at[u, 1], g_r.at[u, 1], d_left)
        cut = gcut(zl, n, n, u)
        gv[cut] = (gv[cut].astype(F32) + r1[1, u, 0:n].astype(F32)).astype(BF)
        send(gv.at[cut], r2.at[1, u, hi], g_s.at[u, 5], g_r.at[u, 5], d_left)

    def grad_ring(u):
        n = 1 if late(u) else 2
        lo, hi = pl.ds(0, n), pl.ds(n, n)
        wait_recv(r2.at[0, u, hi], g_s.at[u, 2], g_r.at[u, 2], d_right)
        wait_recv(r2.at[1, u, lo], g_s.at[u, 3], g_r.at[u, 3], d_left)
        wait_recv(r2.at[0, u, lo], g_s.at[u, 4], g_r.at[u, 4], d_right)
        wait_recv(r2.at[1, u, hi], g_s.at[u, 5], g_r.at[u, 5], d_left)
        own = gv[gcut(z, 0, 2 * n, u)].astype(F32)
        own = own + r2[0, u, 0:2 * n].astype(F32) + r2[1, u, 0:2 * n].astype(F32)
        if late(u):
            sv[u, 0:2] = own.astype(BF)
            send(sv.at[u, 1 - e], pr.at[u], pr_s.at[u], pr_r.at[u], d_pair)
            grad_store(u, h, sv[u, e])
        else:
            sv[u] = own.astype(BF)
            send(sv.at[u, pl.ds(2, 2)], nr.at[u], nb_s.at[u], nb_r.at[u], d_nb)

    def grad_store(u, side, value):
        c, q = u // NQ, u % NQ
        cols = pl.ds(pl.multiple_of(side * HALF + q * QC, QC), QC)
        og_ref[c * 16:(c + 1) * 16, cols] = value

    def grad_pair(u):
        if late(u):
            return
        wait_recv(nr.at[u], nb_s.at[u], nb_r.at[u], d_nb)
        uv[u] = (sv[u, 1 - e].astype(F32) + nr[u, 1 - e].astype(F32)).astype(BF)
        send(uv.at[u], pr.at[u], pr_s.at[u], pr_r.at[u], d_pair)
        grad_store(u, h, (sv[u, e].astype(F32) + nr[u, e].astype(F32)).astype(BF))

    def grad_out(u):
        wait_recv(pr.at[u], pr_s.at[u], pr_r.at[u], d_pair)
        grad_store(u, 1 - h, pr[u])

    sel_r = lax.broadcasted_iota(jnp.int32, (128, 128), 0)
    sel_c = lax.broadcasted_iota(jnp.int32, (128, 128), 1)

    def quantize(fi, own):
        layer = lo_ref[fi]
        side, dst = (core, qo) if own else (1 - core, qs)

        @pl.loop(0, HALF // QT)
        def _(j):
            pick = jnp.where(sel_r == (sel_c | (QB - 1)), 1.0, 0.0).astype(BF)
            for k in range(QT // 128):
                col = pl.ds(pl.multiple_of(j * QT + k * 128, 128), 128)
                a = gv[layer, side, :, col].astype(F32)
                b = gv[fi, 2 + side, :, col].astype(F32)
                drift = a - b
                m = jnp.abs(drift)
                for s in (1, 2, 4, 8, 16):
                    m = jnp.maximum(m, pltpu.roll(m, s, 1))
                sc = jnp.dot((m + scale_eps).astype(BF), pick, preferred_element_type=F32)
                quant = (drift / sc).astype(BF).astype(F32)
                dst[fi, :, col] = (quant * sc).astype(BF)

        if not own:
            send(qs.at[fi], qr.at[fi], q_s.at[fi], q_r.at[fi], d_core)

    def tiles(body):
        @pl.loop(0, HALF // QT)
        def _(j):
            body(pl.ds(pl.multiple_of(j * QT, QT), QT), j)

    def outer_core(fi):
        wait_recv(qr.at[fi], q_s.at[fi], q_r.at[fi], d_core)

        def body(cols, j):
            s2[fi, :, cols] = (qo[fi, :, cols].astype(F32) + qr[fi, :, cols].astype(F32)).astype(BF)

        tiles(body)
        send(s2.at[fi], xr.at[fi], xl_s.at[fi], xl_r.at[fi], d_xlo)

    def outer_x(fi):
        wait_recv(xr.at[fi], xl_s.at[fi], xl_r.at[fi], d_xlo)

        def body(cols, j):
            qo[fi, :, cols] = (s2[fi, :, cols].astype(F32) + xr[fi, :, cols].astype(F32)).astype(BF)

        tiles(body)
        send(qo.at[fi], fr.at[fi], fr_s.at[fi], fr_r.at[fi], d_core)
        write_sum(qo, fi, core, 0)

    def write_sum(src, fi, side, k):
        cols = pl.ds(pl.multiple_of(side * HALF, HALF), HALF)
        c = pltpu.make_async_copy(src.at[fi], os_hbm.at[fi, :, cols], os_sem.at[fi, k])
        c.start()
        written.append(c)

    def outer_end(fi):
        wait_recv(fr.at[fi], fr_s.at[fi], fr_r.at[fi], d_core)
        write_sum(fr, fi, 1 - core, 1)

    written = []

    def in_step():
        pl.semaphore_signal(step_sem, inc=1, device_id=d_core, device_id_type=MESH)
        pl.semaphore_wait(step_sem, 1)

    for r in range(2):
        w_pair_send(r)
        w_nb_send(0, r)
    for r in range(2):
        w_zsend(0, r)
    for t in range(NT):
        x_send(t)
    for c in loads[8:]:
        c.wait()
    quantize(0, False)
    quantize(0, True)
    w_pair_got(0)
    w_nb_send(1, 0)
    w_zsend(1, 0)
    w_nb_got(0, 0)
    w_zsend(2, 0)
    w_pair_got(1)
    w_nb_send(1, 1)
    w_fwd(0, 0)
    quantize(1, False)
    quantize(1, True)
    w_zsend(1, 1)
    w_nb_got(1, 0)
    w_zsend(3, 0)
    w_nb_got(0, 1)
    w_zsend(2, 1)
    w_fwd(0, 1)
    quantize(2, False)
    quantize(2, True)
    w_nb_got(1, 1)
    w_zsend(3, 1)
    w_fwd(1, 0)
    w_fwd(2, 0)
    for fi in range(FRAG):
        outer_core(fi)
    cp_t.wait()
    for c in range(NCH):
        targets_chunk(c)
    w_fwd(3, 0)
    w_fwd(1, 1)
    for p in range(4):
        w_end(p, 0)
    cp_x.wait()
    key_own(0)
    key_own(1)
    w_fwd(2, 1)
    x_got(0)
    key_pair(0, 0)
    key_pair(1, 0)
    w_fwd(3, 1)
    key_mid(0, 0)
    key_mid(1, 0)
    x_got(1)
    key_pair(0, 1)
    key_pair(1, 1)
    key_res(0, 0)
    key_mid(0, 1)
    for p in range(4):
        w_end(p, 1)
    key_pair(2, 0)
    key_mid(1, 1)
    key_res(0, 1)
    key_pair(2, 1)
    key_own(2)
    key_res(1, 0)
    key_done(0)
    in_step()
    grad_unit(0)
    key_pair(3, 0)
    key_pair(3, 1)
    key_mid(2, 0)
    key_mid(2, 1)
    key_res(1, 1)
    key_own(3)
    in_step()
    grad_unit(1)
    key_mid(3, 0)
    key_mid(3, 1)
    grad_fwd(0)
    key_done(1)
    in_step()
    grad_unit(2)
    key_res(2, 0)
    key_res(2, 1)
    grad_fwd(1)
    grad_ring(0)
    outer_x(0)
    key_res(3, 0)
    key_res(3, 1)
    in_step()
    grad_unit(3)
    key_done(2)
    grad_fwd(2)
    grad_ring(1)
    grad_pair(0)
    in_step()
    grad_unit(5)
    grad_unit(4)
    outer_x(1)
    key_done(3)
    grad_fwd(3)
    grad_ring(2)
    grad_pair(1)
    grad_out(0)
    in_step()
    grad_unit(6)
    grad_unit(7)
    outer_x(2)
    grad_nb(5)
    grad_fwd(4)
    grad_ring(3)
    grad_pair(2)
    grad_out(1)
    in_step()
    grad_nb(6)
    grad_fwd(5)
    grad_ring(4)
    grad_pair(3)
    grad_out(2)
    for fi in range(FRAG):
        outer_end(fi)
    in_step()
    grad_nb(7)
    grad_fwd(6)
    grad_ring(5)
    grad_pair(4)
    grad_out(3)
    grad_fwd(7)
    grad_ring(6)
    grad_out(4)
    grad_out(5)
    grad_ring(7)
    grad_out(6)
    grad_out(7)
    for c in written:
        c.wait()
    for c in started:
        c.wait_send()


def exchange(layer_order, own_layers, outer_base, tokens_in, target_keys):
    vm = pltpu.VMEM
    dma = pltpu.SemaphoreType.DMA
    anyspec = pl.BlockSpec(memory_space=pl.ANY)
    return pl.pallas_call(
        kernel,
        out_shape=(
            jax.ShapeDtypeStruct((64, 2 * HALF), BF),
            jax.ShapeDtypeStruct((FRAG, 64, 2 * HALF), BF),
        ),
        in_specs=[pl.BlockSpec(memory_space=pltpu.SMEM)] + [anyspec] * 4,
        out_specs=(pl.BlockSpec(memory_space=pltpu.VMEM), anyspec),
        scratch_shapes=[
            vm((512, 1024), BF),
            vm((NCH, 256, 512), BF),
            vm((2, 512, HALF), BF),
            vm((4, 4, 64, HALF), BF),
            vm((64, HALF), BF),
            vm((NCH, NT, 256, TT), F32),
            vm((NCH, NT, 256, TT), BF),
            vm((NCH, NT, 256, TT), BF),
            vm((NCH, NT, 256, TT), BF),
            vm((NCH, NT, 256, TT), BF),
            vm((2, NCH, NT, 256, TT), BF),
            vm((4, 4, 64, HALF), BF),
            vm((2, NU, 2, 16, QC), BF),
            vm((2, NU, 4, 16, QC), BF),
            vm((NU, 4, 16, QC), BF),
            vm((NU, 2, 16, QC), BF),
            vm((NU, 16, QC), BF),
            vm((NU, 16, QC), BF),
            vm((NY, 4, 2, 16, QC), BF),
        ]
        + [vm((FRAG, 64, HALF), BF) for _ in range(6)]
        + [
            dma((4,)), dma((2, 4, 2)), dma((FRAG, 2)), pltpu.SemaphoreType.REGULAR,
            dma((2, 4, 4)), dma((2, 4, 4)),
            dma((2,)), dma((2,)),
            dma((2, 2)), dma((2, 2)),
            dma((NT,)), dma((NT,)),
            dma((NCH, NT)), dma((NCH, NT)),
            dma((NCH, NT)), dma((NCH, NT)),
            dma((NCH, NT)), dma((NCH, NT)),
            dma((NU, 6)), dma((NU, 6)),
            dma((NU,)), dma((NU,)),
            dma((NY,)), dma((NY,)),
            dma((NU,)), dma((NU,)),
            dma((FRAG,)), dma((FRAG,)),
            dma((FRAG,)), dma((FRAG,)),
            dma((FRAG,)), dma((FRAG,)),
        ],
        compiler_params=pltpu.CompilerParams(
            collective_id=0, has_side_effects=True, vmem_limit_bytes=48 * 2**20
        ),
    )(layer_order, own_layers, outer_base, tokens_in, target_keys)


def per_device(local_weights, outer_base, momentum, layer_order, features, targets):
    grad, summed = exchange(layer_order, local_weights[0], outer_base, features[0], targets[0])
    mean_drift = summed.astype(F32) / lax.axis_size("island")
    moment_new = outer_mu * momentum + mean_drift
    base_new = (
        outer_base.astype(F32) + outer_rate * (mean_drift + outer_mu * moment_new)
    ).astype(BF)
    return (base_new, moment_new, grad.astype(F32)[None])


def solution(mesh):
    return jax.shard_map(
        per_device,
        mesh=mesh,
        in_specs=(
            P("island", None, "fsdp", "tp"),
            P(None, "fsdp", "tp"),
            P(None, "fsdp", "tp"),
            P(),
            P("island", "fsdp", "tp"),
            P("island", "fsdp", None),
        ),
        out_specs=(P(None, "fsdp", "tp"), P(None, "fsdp", "tp"), P("island", "fsdp", "tp")),
        check_vma=False,
    )
```
